32 devices in a mesh: groups: 2 (over y), dp: 8 (over z, core), vocab: 2 (over x).
Axes of the slice: x: 2, y: 2, z: 4, core: 2. Of those that a mesh axis runs over, the one named last changes fastest.
Arguments:
- teacher_hidden: bfloat16 [128, 5120], P(('groups', 'dp')), parts along dimension 0, may hold values from -110 to 110
- teacher_head: bfloat16 [5120, 98304], P(None, ('dp', 'vocab')), may hold values from -0.078125 to 0.078125
- map_dest: int32 [768, 4], P(('dp', 'vocab')), may hold values from 0 to 7, all different within a row; in each aligned block of 48 rows (0 to 47, 48 to 95, ...) at most 24 rows name the same one
- map_slot: int32 [768, 4], P(('dp', 'vocab')), may hold values from 0 to 31
- map_weight: bfloat16 [768, 4, 128, 128], P(('dp', 'vocab')), may hold values from 0.019897461 to 1
- student_hidden: bfloat16 [128, 4096], P(('groups', 'dp')), parts along dimension 0, may hold values from -110 to 110
- student_head: bfloat16 [4096, 65536], P(None, ('dp', 'vocab')), may hold values from -0.09375 to 0.09375
- targets: int32 [128], P(('groups', 'dp')), parts along dimension 0, may hold values from 0 to 65535
Outputs:
- grad_hidden: bfloat16 [128, 4096], P(('groups', 'dp', 'vocab')), parts along dimension 0
The draws below stay inside these ranges and needn't reach their ends.
There are 2 independent parts, one for each index of `groups`. The reference program is written for one: setup_inputs(seed, part) draws one part's arguments, and reference() takes and returns one part's arrays. A program takes and returns all parts, laid end to end along the dimension named above; an argument that names none is the same for every part. Nothing has to cross between parts.
Inputs may be any that keep to these rules, and one draw needn't show every extreme that they name: `map_dest`: the 4 entries of a row differ. Among the 48 rows of one device (aligned blocks of rows) no value appears more than 24 times, and some value appears exactly 24 times.
All inputs are finite; a program needn't handle non-finite values.
Results may differ from the reference program's by a relative error of at most 0.012.
Values may be sent and summed in bfloat16 or wider, within the bound.
A program may use at most 192 MiB of HBM per device.

```python
import math
import jax
import jax.numpy as jnp
import numpy as np
from jax import lax

DT = 5120
DS = 4096
VT = 98304
VS = 65536
BLOCK = 128
R = 4
TOKENS = 64
NTB = 768
TBLK_DEV = 48
SBLK_DEV = 32
CAP = 24
N_DP = 8
N_VOCAB = 2


def hidden_draw(key, rows, width):
    base_key, scale_key = jax.random.split(key, 2)
    scales = jnp.exp(jax.random.uniform(scale_key, (rows, 1), jnp.float32, math.log(2.0), math.log(16.0)))
    values = jnp.clip(jax.random.normal(base_key, (rows, width), jnp.float32), -6.0, 6.0)
    return (values * scales).astype(jnp.bfloat16)


def draw_teacher_hidden(key, part):
    return hidden_draw(jax.random.fold_in(key, 11), TOKENS, DT)


def draw_student_hidden(key, part):
    return hidden_draw(jax.random.fold_in(key, 23), TOKENS, DS)


def plant(values, key, low, high):
    longest = values.shape.index(max(values.shape))
    spots = []
    for shift in (0, 1):
        where = [jax.random.randint(jax.random.fold_in(key, axis), (), 0, length) for axis, length in enumerate(values.shape)]
        where[longest] = (where[longest] + shift) % values.shape[longest]
        spots.append(tuple(where))
    return values.at[spots[0]].set(low).at[spots[1]].set(high)


def block_levels(stream_key, extent, cuts, smallest, largest):
    def one(dim, parts):
        heights = jax.random.uniform(jax.random.fold_in(jax.random.fold_in(stream_key, 6), dim), (parts,), jnp.float32, smallest / len(cuts), largest / len(cuts))
        return jnp.repeat(jnp.exp(heights), extent[dim] // parts).reshape((-1,) + (1,) * (len(extent) - dim - 1))

    gain = one(*cuts[0])
    for cut in cuts[1:]:
        gain = gain * one(*cut)
    return gain


def cumulative_ranks(count, skew):
    loads = [(1 << 20) // math.isqrt(standing ** skew) + 1 for standing in range(1, count + 1)]
    spread = 1 + sum(loads) // (1 << 30)
    return np.cumsum(np.array([max(1, weight // spread) for weight in loads]))


def skewed_ids(stream_key, dims, number_of, slope):
    grid = cumulative_ranks(number_of, slope)
    lot = jax.random.randint(jax.random.fold_in(stream_key, 1), dims, 0, int(grid[number_of - 1]))
    standing = jnp.searchsorted(jnp.asarray(grid, jnp.int32), lot, side="right")
    return jax.random.permutation(jax.random.fold_in(stream_key, 2), number_of)[standing].astype(jnp.int32)


def assign_block(stream_key, own, number, rows, count, top, bound, skew):
    order = jax.random.permutation(stream_key, count)
    packed, ordinary = load_shares(count, rows * top, bound, skew, True), load_shares(count, rows * top, bound, skew, False)
    places = jnp.arange(count)

    def named(tallies, rotation):
        used = int((tallies > 0).sum())
        fixed = max(1, used // 4)
        moved = fixed + (places - fixed + rotation * (used - fixed)) % max(1, count - fixed)
        return jnp.zeros((count,), jnp.int32).at[order[jnp.where(places < fixed, places, moved)]].set(jnp.asarray(tallies, jnp.int32))

    tallies = jnp.where(number % 4 == 0, named(packed, number // 4), named(ordinary, number - number // 4 - 1))
    mixed = jax.random.permutation(jax.random.fold_in(own, 3), count)
    donor, sink = mixed[0:count // 2 * 2:2], mixed[1:count // 2 * 2:2]
    margin = jnp.minimum(tallies[donor] - 1, bound - tallies[sink]) // 2
    margin = jnp.where((donor == order[0]) | (sink == order[0]) | (tallies[sink] == 0), 0, jnp.maximum(margin, 0))
    moved = jax.random.randint(jax.random.fold_in(own, 4), (count // 2,), 0, 1 << 20) % (margin + 1)
    tallies = tallies.at[donor].add(-moved).at[sink].add(moved)
    members = jnp.searchsorted(jnp.cumsum(tallies), jnp.arange(rows * top), side="right").astype(jnp.int32)
    listing = members.reshape(top, rows).T
    listing = listing[jax.random.permutation(jax.random.fold_in(own, 1), rows)]
    rotation = jax.random.randint(jax.random.fold_in(own, 2), (rows, 1), 0, top)
    return jnp.take_along_axis(listing, (jnp.arange(top)[None, :] + rotation) % top, axis=1)


def load_shares(amount, total, reach, skew, full):
    portions = [(1 << 20) // math.isqrt(grade ** skew) + 1 for grade in range(1, amount + 1)]
    largest = reach if full else min(reach, max(-(-total // amount), total * portions[0] // sum(portions)))
    least = 1 if total - largest >= amount - 1 else 0
    given, rest = [largest] + [least] * (amount - 1), total - largest - least * (amount - 1)
    while rest > 0:
        candidates = [i for i in range(1, amount) if given[i] < largest] or [i for i in range(1, amount) if given[i] < reach]
        mass, budget = sum([portions[i] for i in candidates]), rest
        for i in candidates:
            extra = min(reach - given[i], max(1, budget * portions[i] // mass), rest)
            given[i] = given[i] + extra
            rest = rest - extra
    return np.array(given)


def centred(own_key, dims, scale, most, shards=(), kind=jnp.bfloat16):
    result = jax.random.normal(own_key, dims, jnp.float32) * scale
    if len(shards) > 0:
        result = block_levels(own_key, dims, shards, -0.22, 0.18) * result
    return jnp.clip(result, min=-most, max=most).astype(kind)


def setup_inputs(seed: int = 0, part: int = 0) -> dict:
    keys = jax.random.split(jax.random.key(seed), 9)
    part_splits = jax.random.split(jax.random.fold_in(keys[8], part), 9)
    teacher_hidden = draw_teacher_hidden(jax.random.fold_in(jax.random.fold_in(keys[8], part), 71), part)
    teacher_head = centred(keys[1], (DT, VT), DT ** -0.5, 0.078125, ((1, 16),))
    map_dest_keys = jax.random.split(jax.random.fold_in(keys[2], 1), NTB // TBLK_DEV)
    map_dest_turns = jax.random.permutation(jax.random.fold_in(keys[2], 3), NTB // TBLK_DEV)
    map_dest = jax.vmap(lambda own, number: assign_block(jax.random.fold_in(keys[2], 2), own, number, TBLK_DEV, N_DP, R, CAP, 2))(map_dest_keys, map_dest_turns).reshape((NTB, R))
    map_slot = plant(jax.random.randint(keys[3], (NTB, R), 0, SBLK_DEV), jax.random.fold_in(keys[3], 1), 0, SBLK_DEV - 1).astype(jnp.int32)
    map_weight = jnp.clip(jnp.exp(math.log(1.0) - 3.9171631 * jax.random.uniform(keys[4], (NTB, R, BLOCK, BLOCK), jnp.float32) ** block_levels(keys[4], (NTB, R, BLOCK, BLOCK), ((0, 16),), -0.2, 0.2)), 0.019897461, 1.0).astype(jnp.bfloat16)
    student_hidden = draw_student_hidden(jax.random.fold_in(jax.random.fold_in(keys[8], part), 71), part)
    student_head = centred(keys[6], (DS, VS), DS ** -0.5, 0.09375, ((1, 16),))
    targets = plant(skewed_ids(part_splits[7], (TOKENS,), VS, 2), jax.random.fold_in(part_splits[7], 3), 0, VS - 1).astype(jnp.int32)
    return {"teacher_hidden": teacher_hidden, "teacher_head": teacher_head, "map_dest": map_dest, "map_slot": map_slot, "map_weight": map_weight, "student_hidden": student_hidden, "student_head": student_head, "targets": targets}


hard_weight = 0.25
loss_scale = 64.0


def reference(teacher_hidden, teacher_head, map_dest, map_slot, map_weight, student_hidden, student_head, targets):
    teacher_logits = jnp.dot(teacher_hidden, teacher_head, preferred_element_type=jnp.float32)
    teacher_peak = jnp.max(teacher_logits, axis=1, keepdims=True)
    teacher_weights = jnp.exp(teacher_logits - teacher_peak).astype(jnp.bfloat16)
    prob_blocks = jnp.transpose(teacher_weights.reshape(TOKENS, VT // BLOCK, BLOCK), (1, 0, 2))
    teacher_coord = (jnp.arange(VT // BLOCK, dtype=jnp.int32) // TBLK_DEV) % N_VOCAB
    dest_block = ((map_dest * N_VOCAB + teacher_coord[:, None]) * SBLK_DEV + map_slot).astype(jnp.int32)

    def accumulate(mapped, scan_item):
        prob_block, weight_block, block_ids = scan_item
        mapped_terms = jnp.einsum("tc,rcd->rtd", prob_block.astype(jnp.float32), weight_block.astype(jnp.float32))
        rounded = lax.optimization_barrier(mapped_terms.astype(jnp.bfloat16))
        return mapped.at[block_ids].add(rounded.astype(jnp.float32)), None

    start_mapped = jnp.zeros((VS // BLOCK, TOKENS, BLOCK), jnp.float32)
    mapped, unused_out = lax.scan(accumulate, start_mapped, (prob_blocks, map_weight, dest_block))
    mapped = jnp.transpose(mapped, (1, 0, 2)).reshape(TOKENS, VS)
    target_total = jnp.sum(mapped, axis=1, keepdims=True)
    target_probs = mapped / target_total
    student_logits = jnp.dot(student_hidden, student_head, preferred_element_type=jnp.float32)
    student_peak = jnp.max(student_logits, axis=1, keepdims=True)
    student_exp = jnp.exp(student_logits - student_peak)
    student_probs = student_exp / jnp.sum(student_exp, axis=1, keepdims=True)
    target_hits = (jnp.arange(VS, dtype=jnp.int32)[None, :] == targets[:, None]).astype(jnp.float32)
    logit_grad = (loss_scale * (student_probs - (1.0 - hard_weight) * target_probs - hard_weight * target_hits)).astype(jnp.bfloat16)
    gradient = jnp.dot(logit_grad, student_head.T, preferred_element_type=jnp.float32)
    return gradient.astype(jnp.bfloat16)
```

```python
import functools

import jax
import jax.numpy as jnp
from jax import lax
from jax.experimental import pallas as pl
from jax.experimental.pallas import tpu as pltpu
from jax.sharding import PartitionSpec as P

MESH = pl.DeviceIdType.MESH
hard_weight = 0.25
loss_scale = 64.0
vmem_bytes = 60 * 1024 * 1024


def chunk_of(cols):
    for size in (512, 256, 128):
        if cols % size == 0:
            return size
    return cols


def teacher_kernel(
    chips, own_t, own_s, own_id, head, logits, all_s, all_id,
    held_t, held_s, held_id, tiles, tile_sem, send_sem, recv_sem, pass_sem, land_sem,
):
    place = lax.axis_index("dp")
    chip, core = place // 2, place % 2
    slots, width = tiles.shape[0], tiles.shape[2]
    steps = head.shape[1] // width

    def fetch(step, slot):
        return pltpu.make_async_copy(
            head.at[:, pl.ds(pl.multiple_of(step * width, width), width)],
            tiles.at[slot],
            tile_sem.at[slot],
        )

    for slot in range(min(slots, steps)):
        fetch(slot, slot).start()
    held_t[place] = own_t[...]
    held_s[place] = own_s[...]
    held_id[place] = own_id[...]

    barrier = pltpu.get_barrier_semaphore()
    partner = chip * 2 + (1 - core)
    for hop in range(1, chips):
        other = (chip + hop) % chips * 2 + core
        pl.semaphore_signal(barrier, inc=1, device_id={"dp": other}, device_id_type=MESH)
    pl.semaphore_signal(barrier, inc=1, device_id={"dp": partner}, device_id_type=MESH)
    pl.semaphore_wait(barrier, chips)

    helds = (held_t, held_id, held_s)

    def across(kind, hop):
        return pltpu.make_async_remote_copy(
            src_ref=helds[kind].at[place],
            dst_ref=helds[kind].at[place],
            send_sem=send_sem.at[kind, hop],
            recv_sem=recv_sem.at[kind, hop],
            device_id={"dp": (chip + hop) % chips * 2 + core},
            device_id_type=MESH,
        )

    def between(kind, hop):
        block = (chip + chips - hop) % chips * 2 + core
        return pltpu.make_async_remote_copy(
            src_ref=helds[kind].at[block],
            dst_ref=helds[kind].at[block],
            send_sem=pass_sem.at[kind, hop],
            recv_sem=land_sem.at[kind, hop],
            device_id={"dp": partner},
            device_id_type=MESH,
        )

    for kind in range(3):
        for hop in range(1, chips):
            across(kind, hop).start()
        between(kind, 0).start()
    for hop in range(1, chips):
        across(0, hop).wait_recv()
        between(0, hop).start()
    for hop in range(chips):
        between(0, hop).wait_recv()

    tokens = held_t.shape[0] * held_t.shape[1]

    def multiply(step, carry):
        slot = step % slots
        fetch(step, slot).wait()
        logits[:, pl.ds(pl.multiple_of(step * width, width), width)] = jnp.dot(
            held_t[...].reshape(tokens, held_t.shape[2]),
            tiles[slot],
            preferred_element_type=jnp.float32,
        )

        @pl.when(step + slots < steps)
        def _():
            fetch(step + slots, slot).start()

        return carry

    middle = steps // 2
    lax.fori_loop(0, middle, multiply, 0)
    for kind in (1, 2):
        for hop in range(1, chips):
            across(kind, hop).wait_recv()
            between(kind, hop).start()
    lax.fori_loop(middle, steps, multiply, 0)
    for kind in (1, 2):
        for hop in range(chips):
            between(kind, hop).wait_recv()
    for kind in range(3):
        for hop in range(1, chips):
            across(kind, hop).wait_send()
        for hop in range(chips):
            between(kind, hop).wait_send()
    all_s[...] = held_s[...]
    all_id[...] = held_id[...]


def teacher_call(chips, own_t, own_s, own_id, head):
    depth, cols = head.shape
    width = chunk_of(cols)
    slots = min(8, cols // width)
    places = chips * 2
    rows = own_t.shape[0]
    vmem = pl.BlockSpec(memory_space=pltpu.VMEM)
    return pl.pallas_call(
        functools.partial(teacher_kernel, chips),
        out_shape=(
            jax.ShapeDtypeStruct((places * rows, cols), jnp.float32),
            jax.ShapeDtypeStruct((places,) + own_s.shape, own_s.dtype),
            jax.ShapeDtypeStruct((places,) + own_id.shape, own_id.dtype),
        ),
        in_specs=[vmem, vmem, vmem, pl.BlockSpec(memory_space=pl.ANY)],
        out_specs=(vmem, vmem, vmem),
        scratch_shapes=[
            pltpu.VMEM((places,) + own_t.shape, own_t.dtype),
            pltpu.VMEM((places,) + own_s.shape, own_s.dtype),
            pltpu.VMEM((places,) + own_id.shape, own_id.dtype),
            pltpu.VMEM((slots, depth, width), head.dtype),
            pltpu.SemaphoreType.DMA((slots,)),
            pltpu.SemaphoreType.DMA((3, chips)),
            pltpu.SemaphoreType.DMA((3, chips)),
            pltpu.SemaphoreType.DMA((3, chips)),
            pltpu.SemaphoreType.DMA((3, chips)),
        ],
        compiler_params=pltpu.CompilerParams(
            collective_id=0, has_side_effects=True, vmem_limit_bytes=vmem_bytes
        ),
    )(own_t, own_s, own_id, head)


def student_kernel(
    chips, vocabs, dense, peak_row, all_s, all_id, head, out,
    whole, summed, up_in, down_in, peaks, stats, logits, grad, partial, sent, landed,
    tile_sem, peak_send, peak_recv, stat_send, stat_recv, core_send, core_recv,
    up_send, up_recv, down_send, down_recv, grad_send, grad_recv,
):
    place, vocab = lax.axis_index("dp"), lax.axis_index("vocab")
    chip, core = place // 2, place % 2
    partner = chip * 2 + (1 - core)
    count = chips * 2 * vocabs
    me = place * vocabs + vocab
    blocks, tokens, block = summed.shape[1:]
    depth, cols = head.shape
    width = chunk_of(cols)
    steps = cols // width
    last = chips - 1

    def fetch(step):
        at = pl.ds(pl.multiple_of(step * width, width), width)
        return pltpu.make_async_copy(head.at[:, at], whole.at[:, at], tile_sem.at[step])

    for step in range(steps):
        fetch(step).start()
    peaks[me] = peak_row[...]

    def every(body):
        lax.fori_loop(1, count, lambda hop, carry: (body(hop), carry)[1], 0)

    def peer(hop):
        other = (me + hop) % count
        return {"dp": other // vocabs, "vocab": other % vocabs}

    barrier = pltpu.get_barrier_semaphore()
    every(lambda hop: pl.semaphore_signal(barrier, inc=1, device_id=peer(hop), device_id_type=MESH))
    pl.semaphore_wait(barrier, count - 1)

    def share(ref, send_sem, recv_sem):
        def one(hop):
            return pltpu.make_async_remote_copy(
                src_ref=ref.at[me], dst_ref=ref.at[me],
                send_sem=send_sem.at[hop], recv_sem=recv_sem.at[hop],
                device_id=peer(hop), device_id_type=MESH,
            )
        return one

    share_peak = share(peaks, peak_send, peak_recv)
    share_stat = share(stats, stat_send, stat_recv)
    every(lambda hop: share_peak(hop).start())

    order = []
    for near in range((chips + 1) // 2):
        order += [last - near] + ([near] if near != last - near else [])

    def to_core(target):
        return pltpu.make_async_remote_copy(
            src_ref=dense.at[target * 2 + 1 - core], dst_ref=summed.at[target],
            send_sem=core_send.at[target], recv_sem=core_recv.at[target],
            device_id={"dp": partner}, device_id_type=MESH,
        )

    def up(target):
        return pltpu.make_async_remote_copy(
            src_ref=summed.at[target], dst_ref=up_in.at[target],
            send_sem=up_send.at[target], recv_sem=up_recv.at[target],
            device_id={"dp": (chip + 1) % chips * 2 + core}, device_id_type=MESH,
        )

    def down(target):
        return pltpu.make_async_remote_copy(
            src_ref=summed.at[target], dst_ref=down_in.at[target],
            send_sem=down_send.at[target], recv_sem=down_recv.at[target],
            device_id={"dp": (chip + last) % chips * 2 + core}, device_id_type=MESH,
        )

    for target in order:
        to_core(target).start()

    eye = lax.broadcasted_iota(jnp.int32, (tokens, tokens), 0) == lax.broadcasted_iota(
        jnp.int32, (tokens, tokens), 1
    )

    def column(row):
        return jnp.sum(jnp.where(eye, row, 0.0), axis=1, keepdims=True)

    def row_of(col):
        return jnp.sum(jnp.where(eye, col, 0.0), axis=0, keepdims=True)

    def add_rows(index, total):
        tile = dense[index // blocks, index % blocks]
        return total + tile.astype(jnp.float32)

    row_total = lax.fori_loop(
        0, 2 * chips * blocks, add_rows, jnp.zeros((tokens, block), jnp.float32)
    )
    every(lambda hop: share_peak(hop).wait())
    peak = column(jnp.max(peaks[:, 0:1, :], axis=0))
    own_scale = jnp.exp(column(peaks[me, 0:1, :]) - peak)
    partner_scale = jnp.exp(column(peaks[partner * vocabs + vocab, 0:1, :]) - peak)
    term_total = own_scale * jnp.sum(row_total, axis=1, keepdims=True)
    own_wide = jnp.broadcast_to(own_scale, (tokens, block))
    partner_wide = jnp.broadcast_to(partner_scale, (tokens, block))

    for target in order:
        to_core(target).wait_recv()

        def combine(index, carry):
            summed[target, index] = (
                dense[target * 2 + core, index].astype(jnp.float32) * own_wide
                + summed[target, index].astype(jnp.float32) * partner_wide
            ).astype(summed.dtype)
            return carry

        lax.fori_loop(0, blocks, combine, 0)
        if target > 0:
            @pl.when(chip == 0)
            def _():
                up(target).start()
        if target < last:
            @pl.when(chip == last)
            def _():
                down(target).start()

    def multiply(step, carry):
        fetch(step).wait()
        at = pl.ds(pl.multiple_of(step * width, width), width)
        logits[:, at] = jnp.dot(
            all_s[...].reshape(tokens, depth), whole[:, at], preferred_element_type=jnp.float32
        )
        return carry

    def add_in(target, ref):
        def one(index, carry):
            summed[target, index] = (
                summed[target, index].astype(jnp.float32) + ref[target, index].astype(jnp.float32)
            ).astype(summed.dtype)
            return carry

        lax.fori_loop(0, blocks, one, 0)

    done = 0
    for turn in range(last):
        until = steps if turn == last - 1 else min(steps, (steps + 1) // 2 + turn * (steps // 4))
        lax.fori_loop(done, until, multiply, 0)
        done = until
        high, low = last - turn, turn
        if high > 1:
            @pl.when((chip > 0) & (chip < high))
            def _():
                up(high).wait_recv()
                add_in(high, up_in)
                up(high).start()
        if low < last - 1:
            @pl.when((chip < last) & (chip > low))
            def _():
                down(low).wait_recv()
                add_in(low, down_in)
                down(low).start()

    own_peak = jnp.max(logits[...], axis=1, keepdims=True)
    own_sum = jnp.sum(jnp.exp(logits[...] - own_peak), axis=1, keepdims=True)
    stats[me, 0:1, :] = row_of(term_total)
    stats[me, 1:2, :] = row_of(own_peak)
    stats[me, 2:3, :] = row_of(own_sum)
    stats[me, 3:8, :] = jnp.zeros((5, tokens), jnp.float32)
    every(lambda hop: share_stat(hop).start())
    every(lambda hop: share_stat(hop).wait())
    target_total = column(jnp.sum(stats[:, 0:1, :], axis=0))
    student_peak_row = jnp.max(stats[:, 1:2, :], axis=0)
    student_total = column(
        jnp.sum(stats[:, 2:3, :] * jnp.exp(stats[:, 1:2, :] - student_peak_row), axis=0)
    )
    student_peak = column(student_peak_row)
    student_gain = jnp.broadcast_to(loss_scale / student_total, (tokens, block))
    target_gain = jnp.broadcast_to(loss_scale * (1.0 - hard_weight) / target_total, (tokens, block))
    peak_wide = jnp.broadcast_to(student_peak, (tokens, block))
    ids = all_id[...].reshape(tokens, block)
    lanes = lax.broadcasted_iota(jnp.int32, (tokens, block), 1) + me * cols

    for target in range(chips):
        if target > 0:
            @pl.when(chip == target)
            def _():
                up(target).wait_recv()
        if target < last:
            @pl.when(chip == target)
            def _():
                down(target).wait_recv()

    def finish(index, carry):
        mapped = summed[chip, index].astype(jnp.float32)
        mapped = mapped + jnp.where(chip > 0, up_in[chip, index].astype(jnp.float32), 0.0)
        mapped = mapped + jnp.where(chip < last, down_in[chip, index].astype(jnp.float32), 0.0)
        at = pl.ds(pl.multiple_of(index * block, block), block)
        student = jnp.exp(logits[:, at] - peak_wide) * student_gain
        hits = jnp.where(ids == lanes + index * block, loss_scale * hard_weight, 0.0)
        grad[:, at] = (student - mapped * target_gain - hits).astype(grad.dtype)
        return carry

    lax.fori_loop(0, blocks, finish, 0)

    pieces, span = sent.shape[1] // out.shape[0], sent.shape[2]
    rows = out.shape[0]
    for piece in range(pieces):
        product = lax.dot_general(
            grad[...], whole[piece * span:(piece + 1) * span, :],
            (((1,), (1,)), ((), ())), preferred_element_type=jnp.float32,
        )
        for owner in range(count):
            partial[owner, piece * rows:(piece + 1) * rows, :] = product[owner * rows:(owner + 1) * rows, :]

    def narrow(owner, carry):
        sent[owner] = partial[owner].astype(sent.dtype)
        return carry

    lax.fori_loop(0, count, narrow, 0)

    def share_grad(hop):
        return pltpu.make_async_remote_copy(
            src_ref=sent.at[(me + hop) % count], dst_ref=landed.at[hop],
            send_sem=grad_send.at[hop], recv_sem=grad_recv.at[hop],
            device_id=peer(hop), device_id_type=MESH,
        )

    every(lambda hop: share_grad(hop).start())
    every(lambda hop: share_grad(hop).wait())

    total = lax.fori_loop(
        1, count, lambda hop, total: total + landed[hop].astype(jnp.float32), partial[me]
    )
    for piece in range(pieces):
        out[:, piece * span:(piece + 1) * span] = total[
            piece * rows:(piece + 1) * rows, :
        ].astype(out.dtype)

    for target in range(chips):
        to_core(target).wait_send()
        if target > 0:
            @pl.when(chip < target)
            def _():
                up(target).wait_send()
        if target < last:
            @pl.when(chip > target)
            def _():
                down(target).wait_send()


def student_call(chips, vocabs, dense, peak_row, all_s, all_id, head):
    places, blocks, tokens, block = dense.shape
    count = places * vocabs
    depth, cols = head.shape
    rows = tokens // count
    span = 512
    tall = rows * depth // span
    vmem = pl.BlockSpec(memory_space=pltpu.VMEM)
    dma = pltpu.SemaphoreType.DMA
    return pl.pallas_call(
        functools.partial(student_kernel, chips, vocabs),
        out_shape=jax.ShapeDtypeStruct((rows, depth), jnp.bfloat16),
        in_specs=[vmem, vmem, vmem, vmem, pl.BlockSpec(memory_space=pl.ANY)],
        out_specs=vmem,
        scratch_shapes=[
            pltpu.VMEM((depth, cols), head.dtype),
            pltpu.VMEM((chips, blocks, tokens, block), jnp.bfloat16),
            pltpu.VMEM((chips, blocks, tokens, block), jnp.bfloat16),
            pltpu.VMEM((chips, blocks, tokens, block), jnp.bfloat16),
            pltpu.VMEM((count, 8, tokens), jnp.float32),
            pltpu.VMEM((count, 8, tokens), jnp.float32),
            pltpu.VMEM((tokens, cols), jnp.float32),
            pltpu.VMEM((tokens, cols), jnp.bfloat16),
            pltpu.VMEM((count, tall, span), jnp.float32),
            pltpu.VMEM((count, tall, span), jnp.bfloat16),
            pltpu.VMEM((count, tall, span), jnp.bfloat16),
            dma((cols // chunk_of(cols),)),
            dma((count,)), dma((count,)), dma((count,)), dma((count,)),
            dma((chips,)), dma((chips,)), dma((chips,)), dma((chips,)),
            dma((chips,)), dma((chips,)),
            dma((count,)), dma((count,)),
        ],
        compiler_params=pltpu.CompilerParams(
            collective_id=1, has_side_effects=True, vmem_limit_bytes=vmem_bytes
        ),
    )(dense, peak_row, all_s, all_id, head)


def on_device(
    teacher_hidden, teacher_head, map_dest, map_slot, map_weight,
    student_hidden, student_head, targets,
):
    places = lax.axis_size("dp")
    vocabs = lax.axis_size("vocab")
    chips = places // 2
    block = map_weight.shape[2]
    teacher_blocks, fan = map_dest.shape
    blocks = student_head.shape[1] // block
    wide_ids = jnp.broadcast_to(targets[:, None], (targets.shape[0], block))
    logits, all_s, all_id = teacher_call(chips, teacher_hidden, student_hidden, wide_ids, teacher_head)
    tokens = logits.shape[0]
    peak = jnp.max(logits, axis=1)
    weights = jnp.exp(logits - peak[:, None]).astype(jnp.bfloat16)
    terms = jnp.einsum(
        "gkc,krcd->krgd", weights.reshape(tokens, teacher_blocks, block), map_weight,
        preferred_element_type=jnp.float32,
    ).astype(jnp.bfloat16)
    items = teacher_blocks * fan
    goal = (map_dest * blocks + map_slot).reshape(items)
    marks = (jnp.arange(places * blocks, dtype=jnp.int32)[:, None] == goal[None, :]).astype(jnp.bfloat16)
    dense = jnp.dot(
        marks, terms.reshape(items, tokens * block), preferred_element_type=jnp.float32
    ).astype(jnp.bfloat16).reshape(places, blocks, tokens, block)
    peak_row = jnp.broadcast_to(peak[None, :], (8, tokens))
    return student_call(chips, vocabs, dense, peak_row, all_s, all_id, student_head)


def solution(mesh):
    placed = (
        P(("groups", "dp"), None),
        P(None, ("dp", "vocab")),
        P(("dp", "vocab"), None),
        P(("dp", "vocab"), None),
        P(("dp", "vocab"), None, None, None),
        P(("groups", "dp"), None),
        P(None, ("dp", "vocab")),
        P(("groups", "dp")),
    )
    return jax.shard_map(
        on_device,
        mesh=mesh,
        in_specs=placed,
        out_specs=P(("groups", "dp", "vocab"), None),
        check_vma=False,
    )
```

```python
import functools

import jax
import jax.numpy as jnp
from jax import lax
from jax.experimental import pallas as pl
from jax.experimental.pallas import tpu as pltpu
from jax.sharding import PartitionSpec as P

MESH = pl.DeviceIdType.MESH
hard_weight = 0.25
loss_scale = 64.0
vmem_bytes = 60 * 1024 * 1024


def chunk_of(cols):
    for size in (512, 256, 128):
        if cols % size == 0:
            return size
    return cols


def teacher_kernel(
    chips, own_t, own_s, own_id, head, logits, all_s, all_id, peak_row,
    held_t, held_s, held_id, tiles, tile_sem, send_sem, recv_sem, pass_sem, land_sem,
):
    place = lax.axis_index("dp")
    chip, core = place // 2, place % 2
    slots, width = tiles.shape[0], tiles.shape[2]
    steps = head.shape[1] // width

    def fetch(step, slot):
        return pltpu.make_async_copy(
            head.at[:, pl.ds(pl.multiple_of(step * width, width), width)],
            tiles.at[slot],
            tile_sem.at[slot],
        )

    for slot in range(min(slots, steps)):
        fetch(slot, slot).start()
    held_t[place] = own_t[...]
    held_s[place] = own_s[...]
    rows = own_t.shape[0]
    same = lax.broadcasted_iota(jnp.int32, (rows, rows), 0) == lax.broadcasted_iota(
        jnp.int32, (rows, rows), 1
    )
    held_id[place] = jnp.broadcast_to(
        jnp.sum(jnp.where(same, own_id[...], 0), axis=1, keepdims=True), held_id.shape[1:]
    )

    barrier = pltpu.get_barrier_semaphore()
    partner = chip * 2 + (1 - core)
    for hop in range(1, chips):
        other = (chip + hop) % chips * 2 + core
        pl.semaphore_signal(barrier, inc=1, device_id={"dp": other}, device_id_type=MESH)
    pl.semaphore_signal(barrier, inc=1, device_id={"dp": partner}, device_id_type=MESH)
    pl.semaphore_wait(barrier, chips)

    helds = (held_t, held_id, held_s)

    def across(kind, hop):
        return pltpu.make_async_remote_copy(
            src_ref=helds[kind].at[place],
            dst_ref=helds[kind].at[place],
            send_sem=send_sem.at[kind, hop],
            recv_sem=recv_sem.at[kind, hop],
            device_id={"dp": (chip + hop) % chips * 2 + core},
            device_id_type=MESH,
        )

    def between(kind, hop):
        block = (chip + chips - hop) % chips * 2 + core
        return pltpu.make_async_remote_copy(
            src_ref=helds[kind].at[block],
            dst_ref=helds[kind].at[block],
            send_sem=pass_sem.at[kind, hop],
            recv_sem=land_sem.at[kind, hop],
            device_id={"dp": partner},
            device_id_type=MESH,
        )

    for kind in range(3):
        for hop in range(1, chips):
            across(kind, hop).start()
        between(kind, 0).start()
    for hop in range(1, chips):
        across(0, hop).wait_recv()
        between(0, hop).start()
    for hop in range(chips):
        between(0, hop).wait_recv()

    tokens = held_t.shape[0] * held_t.shape[1]

    def multiply(step, carry):
        slot = step % slots
        fetch(step, slot).wait()
        value = jnp.dot(
            held_t[...].reshape(tokens, held_t.shape[2]),
            tiles[slot],
            preferred_element_type=jnp.float32,
        )
        logits[:, pl.ds(pl.multiple_of(step * width, width), width)] = value
        for start in range(0, width, 128):
            carry = jnp.maximum(carry, value[:, start:start + 128])

        @pl.when(step + slots < steps)
        def _():
            fetch(step + slots, slot).start()

        return carry

    middle = steps // 2
    highest = jnp.full((tokens, 128), -jnp.inf, jnp.float32)
    highest = lax.fori_loop(0, middle, multiply, highest)
    for kind in (1, 2):
        for hop in range(1, chips):
            across(kind, hop).wait_recv()
            between(kind, hop).start()
    highest = lax.fori_loop(middle, steps, multiply, highest)
    for kind in (1, 2):
        for hop in range(chips):
            between(kind, hop).wait_recv()
    for kind in range(3):
        for hop in range(1, chips):
            across(kind, hop).wait_send()
        for hop in range(chips):
            between(kind, hop).wait_send()
    all_s[...] = held_s[...]
    all_id[...] = held_id[...]
    diagonal = lax.broadcasted_iota(jnp.int32, (tokens, tokens), 0) == lax.broadcasted_iota(
        jnp.int32, (tokens, tokens), 1
    )
    peak = jnp.max(highest, axis=1, keepdims=True)
    peak_row[...] = jnp.broadcast_to(
        jnp.sum(jnp.where(diagonal, peak, 0.0), axis=0, keepdims=True), peak_row.shape
    )


def teacher_call(chips, own_t, own_s, own_id, head):
    depth, cols = head.shape
    width = chunk_of(cols)
    slots = min(8, cols // width)
    places = chips * 2
    rows = own_t.shape[0]
    vmem = pl.BlockSpec(memory_space=pltpu.VMEM)
    return pl.pallas_call(
        functools.partial(teacher_kernel, chips),
        out_shape=(
            jax.ShapeDtypeStruct((places * rows, cols), jnp.float32),
            jax.ShapeDtypeStruct((places,) + own_s.shape, own_s.dtype),
            jax.ShapeDtypeStruct((places, rows, 128), own_id.dtype),
            jax.ShapeDtypeStruct((8, places * rows), jnp.float32),
        ),
        in_specs=[vmem, vmem, vmem, pl.BlockSpec(memory_space=pl.ANY)],
        out_specs=(vmem, vmem, vmem, vmem),
        scratch_shapes=[
            pltpu.VMEM((places,) + own_t.shape, own_t.dtype),
            pltpu.VMEM((places,) + own_s.shape, own_s.dtype),
            pltpu.VMEM((places, rows, 128), own_id.dtype),
            pltpu.VMEM((slots, depth, width), head.dtype),
            pltpu.SemaphoreType.DMA((slots,)),
            pltpu.SemaphoreType.DMA((3, chips)),
            pltpu.SemaphoreType.DMA((3, chips)),
            pltpu.SemaphoreType.DMA((3, chips)),
            pltpu.SemaphoreType.DMA((3, chips)),
        ],
        compiler_params=pltpu.CompilerParams(
            collective_id=0, has_side_effects=True, vmem_limit_bytes=vmem_bytes
        ),
    )(own_t, own_s, own_id, head)


def student_kernel(
    chips, vocabs, dense, peak_row, all_s, all_id, head, out,
    whole, summed, up_in, down_in, peaks, stats, logits, grad, product, partial, sent, given, landed,
    tile_sem, peak_send, peak_recv, stat_send, stat_recv, core_send, core_recv,
    up_send, up_recv, down_send, down_recv, give_send, give_recv, grad_send, grad_recv,
):
    place, vocab = lax.axis_index("dp"), lax.axis_index("vocab")
    chip, core = place // 2, place % 2
    partner = chip * 2 + (1 - core)
    count = chips * 2 * vocabs
    me = place * vocabs + vocab
    blocks, tokens, block = summed.shape[1:]
    depth, cols = head.shape
    width = chunk_of(cols)
    steps = cols // width
    last = chips - 1
    parts = core_send.shape[0]
    share_of = blocks // parts

    def fetch(step):
        at = pl.ds(pl.multiple_of(step * width, width), width)
        return pltpu.make_async_copy(head.at[:, at], whole.at[:, at], tile_sem.at[step])

    for step in range(steps):
        fetch(step).start()
    peaks[me] = peak_row[...]

    def every(body):
        lax.fori_loop(1, count, lambda hop, carry: (body(hop), carry)[1], 0)

    def peer(hop):
        other = (me + hop) % count
        return {"dp": other // vocabs, "vocab": other % vocabs}

    barrier = pltpu.get_barrier_semaphore()
    every(lambda hop: pl.semaphore_signal(barrier, inc=1, device_id=peer(hop), device_id_type=MESH))
    pl.semaphore_wait(barrier, count - 1)

    def share(ref, send_sem, recv_sem):
        def one(hop):
            return pltpu.make_async_remote_copy(
                src_ref=ref.at[me], dst_ref=ref.at[me],
                send_sem=send_sem.at[hop], recv_sem=recv_sem.at[hop],
                device_id=peer(hop), device_id_type=MESH,
            )
        return one

    share_peak = share(peaks, peak_send, peak_recv)
    share_stat = share(stats, stat_send, stat_recv)
    every(lambda hop: share_peak(hop).start())

    order = []
    for near in range((chips + 1) // 2):
        order += [last - near] + ([near] if near != last - near else [])

    def to_core(part, target):
        return pltpu.make_async_remote_copy(
            src_ref=dense.at[target * 2 + 1 - core, pl.ds(part * share_of, share_of)],
            dst_ref=summed.at[target, pl.ds(part * share_of, share_of)],
            send_sem=core_send.at[part, target], recv_sem=core_recv.at[part, target],
            device_id={"dp": partner}, device_id_type=MESH,
        )

    def up(part, target):
        return pltpu.make_async_remote_copy(
            src_ref=summed.at[target, pl.ds(part * share_of, share_of)],
            dst_ref=up_in.at[target, pl.ds(part * share_of, share_of)],
            send_sem=up_send.at[part, target], recv_sem=up_recv.at[part, target],
            device_id={"dp": (chip + 1) % chips * 2 + core}, device_id_type=MESH,
        )

    def down(part, target):
        return pltpu.make_async_remote_copy(
            src_ref=summed.at[target, pl.ds(part * share_of, share_of)],
            dst_ref=down_in.at[target, pl.ds(part * share_of, share_of)],
            send_sem=down_send.at[part, target], recv_sem=down_recv.at[part, target],
            device_id={"dp": (chip + last) % chips * 2 + core}, device_id_type=MESH,
        )

    for part in range(parts):
        for target in order:
            to_core(part, target).start()

    eye = lax.broadcasted_iota(jnp.int32, (tokens, tokens), 0) == lax.broadcasted_iota(
        jnp.int32, (tokens, tokens), 1
    )

    def column(row):
        return jnp.sum(jnp.where(eye, row, 0.0), axis=1, keepdims=True)

    def row_of(col):
        return jnp.sum(jnp.where(eye, col, 0.0), axis=0, keepdims=True)

    def add_rows(index, total):
        tile = dense[index // blocks, index % blocks]
        return total + tile.astype(jnp.float32)

    row_total = lax.fori_loop(
        0, 2 * chips * blocks, add_rows, jnp.zeros((tokens, block), jnp.float32)
    )
    every(lambda hop: share_peak(hop).wait())
    peak = column(jnp.max(peaks[:, 0:1, :], axis=0))
    own_scale = jnp.exp(column(peaks[me, 0:1, :]) - peak)
    partner_scale = jnp.exp(column(peaks[partner * vocabs + vocab, 0:1, :]) - peak)
    term_total = own_scale * jnp.sum(row_total, axis=1, keepdims=True)
    own_wide = jnp.broadcast_to(own_scale, (tokens, block))
    partner_wide = jnp.broadcast_to(partner_scale, (tokens, block))

    def combine(part):
        for target in order:
            to_core(part, target).wait_recv()

            def one(index, carry):
                summed[target, index] = (
                    dense[target * 2 + core, index].astype(jnp.float32) * own_wide
                    + summed[target, index].astype(jnp.float32) * partner_wide
                ).astype(summed.dtype)
                return carry

            lax.fori_loop(part * share_of, (part + 1) * share_of, one, 0)

    def multiply(step, carry):
        fetch(step).wait()
        at = pl.ds(pl.multiple_of(step * width, width), width)
        logits[:, at] = jnp.dot(
            all_s[...].reshape(tokens, depth), whole[:, at], preferred_element_type=jnp.float32
        )
        return carry

    def add_in(part, target, ref):
        def one(index, carry):
            summed[target, index] = (
                summed[target, index].astype(jnp.float32) + ref[target, index].astype(jnp.float32)
            ).astype(summed.dtype)
            return carry

        lax.fori_loop(part * share_of, (part + 1) * share_of, one, 0)

    turns = [(part, turn) for part in range(parts) for turn in range(last)]

    def hop_up(at):
        part, high = turns[at][0], last - turns[at][1]

        @pl.when(chip == 0)
        def _():
            if at >= 2:
                up(turns[at - 2][0], last - turns[at - 2][1]).wait_send()
            up(part, high).start()

        if high > 1:
            @pl.when((chip > 0) & (chip < high))
            def _():
                up(part, high).wait_recv()
                add_in(part, high, up_in)
                up(part, high).start()

    def hop_down(at):
        part, low = turns[at]

        @pl.when(chip == last)
        def _():
            if at >= 2:
                down(*turns[at - 2]).wait_send()
            down(part, low).start()

        if low < last - 1:
            @pl.when((chip < last) & (chip > low))
            def _():
                down(part, low).wait_recv()
                add_in(part, low, down_in)
                down(part, low).start()

    def hop(at):
        pl.when(chip * 2 < chips)(lambda: hop_up(at))
        hop_down(at)
        pl.when(chip * 2 >= chips)(lambda: hop_up(at))

    ids = all_id[...].reshape(tokens, block)
    lanes = lax.broadcasted_iota(jnp.int32, (tokens, block), 1) + me * cols

    def totals():
        target_total = column(jnp.sum(stats[:, 0:1, :], axis=0))
        peak_all = jnp.max(stats[:, 1:2, :], axis=0)
        student_total = column(
            jnp.sum(stats[:, 2:3, :] * jnp.exp(stats[:, 1:2, :] - peak_all), axis=0)
        )
        return tuple(
            jnp.broadcast_to(value, (tokens, block))
            for value in (
                column(peak_all),
                loss_scale / student_total,
                loss_scale * (1.0 - hard_weight) / target_total,
            )
        )

    halves = partial.shape[0]
    rows, span = out.shape[0], partial.shape[3]
    pieces = depth // span
    per_half = pieces // halves

    def finish(part, wide):
        peak_wide, student_gain, target_gain = wide
        for target in range(chips):
            if target > 0:
                @pl.when(chip == target)
                def _():
                    up(part, target).wait_recv()
            if target < last:
                @pl.when(chip == target)
                def _():
                    down(part, target).wait_recv()

        def one(index, carry):
            mapped = summed[chip, index].astype(jnp.float32)
            mapped = mapped + jnp.where(chip > 0, up_in[chip, index].astype(jnp.float32), 0.0)
            mapped = mapped + jnp.where(chip < last, down_in[chip, index].astype(jnp.float32), 0.0)
            at = pl.ds(pl.multiple_of(index * block, block), block)
            student = jnp.exp(logits[:, at] - peak_wide) * student_gain
            hits = jnp.where(ids == lanes + index * block, loss_scale * hard_weight, 0.0)
            grad[:, at] = (student - mapped * target_gain - hits).astype(grad.dtype)
            return carry

        lax.fori_loop(part * share_of, (part + 1) * share_of, one, 0)

    def piece_of(part, piece):
        across = slice(part * share_of * block, (part + 1) * share_of * block)
        return lax.dot_general(
            grad[:, across], whole[piece * span:(piece + 1) * span, across],
            (((1,), (1,)), ((), ())), preferred_element_type=jnp.float32,
        )

    def accumulate(part):
        for piece in range(pieces):
            at = slice(piece * span, (piece + 1) * span)
            value = piece_of(part, piece)
            product[:, at] = value if part == 0 else product[:, at] + value

    def give(half, target):
        return pltpu.make_async_remote_copy(
            src_ref=sent.at[half, pl.ds((target * 2 + 1 - core) * vocabs, vocabs)],
            dst_ref=given.at[half, target],
            send_sem=give_send.at[half, target], recv_sem=give_recv.at[half, target],
            device_id={"dp": partner}, device_id_type=MESH,
        )

    column_me = chip * vocabs + vocab
    column_count = chips * vocabs

    def owner_of(step):
        other = (column_me + step) % column_count
        return other // vocabs, other % vocabs

    def share_grad(half, step):
        target, side = owner_of(step)
        return pltpu.make_async_remote_copy(
            src_ref=sent.at[half, (target * 2 + core) * vocabs + side], dst_ref=landed.at[half, step],
            send_sem=grad_send.at[half, step], recv_sem=grad_recv.at[half, step],
            device_id={"dp": target * 2 + core, "vocab": side}, device_id_type=MESH,
        )

    combine(0)
    busy = max(1, (len(turns) + 1) // 2)
    done = 0
    wide = None
    accumulated = 0
    for at, (part, turn) in enumerate(turns):
        hop(at)
        if at < busy:
            until = steps * (at + 1) // busy
            lax.fori_loop(done, until, multiply, 0)
            done = until
        if at == busy - 1:
            own_peak = jnp.max(logits[...], axis=1, keepdims=True)
            own_sum = jnp.sum(jnp.exp(logits[...] - own_peak), axis=1, keepdims=True)
            stats[me, 0:1, :] = row_of(term_total)
            stats[me, 1:2, :] = row_of(own_peak)
            stats[me, 2:3, :] = row_of(own_sum)
            stats[me, 3:8, :] = jnp.zeros((5, tokens), jnp.float32)
            every(lambda step: share_stat(step).start())
        if turn == last - 1 and part + 1 < parts:
            combine(part + 1)
        if at >= busy + last - 1 and at < len(turns) - 1 and accumulated < part:
            if wide is None:
                every(lambda step: share_stat(step).wait())
                wide = totals()
            finish(accumulated, wide)
            accumulate(accumulated)
            accumulated += 1
    if wide is None:
        every(lambda step: share_stat(step).wait())
        wide = totals()
    for part in range(accumulated, parts - 1):
        finish(part, wide)
        accumulate(part)
    finish(parts - 1, wide)

    for half in range(halves):
        for inner in range(per_half):
            piece = half * per_half + inner
            value = piece_of(parts - 1, piece)
            if parts > 1:
                value = value + product[:, piece * span:(piece + 1) * span]
            for owner in range(count):
                partial[half, owner, inner * rows:(inner + 1) * rows, :] = value[owner * rows:(owner + 1) * rows, :]
        for target in range(chips):
            first = (target * 2 + 1 - core) * vocabs
            for side in range(vocabs):
                sent[half, first + side] = partial[half, first + side].astype(sent.dtype)
            give(half, target).start()

    for half in range(halves):
        for target in range(chips):
            give(half, target).wait_recv()

        def pass_on(step, carry):
            target, side = owner_of(step)
            owner = (target * 2 + core) * vocabs + side
            sent[half, owner] = (
                partial[half, owner] + given[half, target, side].astype(jnp.float32)
            ).astype(sent.dtype)
            share_grad(half, step).start()
            return carry

        lax.fori_loop(1, column_count, pass_on, 0)

    for half in range(halves):
        def arrive(step, total):
            share_grad(half, step).wait_recv()
            return total + landed[half, step].astype(jnp.float32)

        total = lax.fori_loop(
            1, column_count, arrive, partial[half, me] + given[half, chip, vocab].astype(jnp.float32)
        )
        for inner in range(per_half):
            piece = half * per_half + inner
            out[:, piece * span:(piece + 1) * span] = total[
                inner * rows:(inner + 1) * rows, :
            ].astype(out.dtype)

    for half in range(halves):
        for target in range(chips):
            give(half, target).wait_send()
        lax.fori_loop(1, column_count, lambda step, carry: (share_grad(half, step).wait_send(), carry)[1], 0)
    for at, (part, turn) in enumerate(turns):
        high, low = last - turn, turn
        late = at >= len(turns) - 2

        @pl.when((chip < high) if late else ((chip > 0) & (chip < high)))
        def _():
            up(part, high).wait_send()

        @pl.when((chip > low) if late else ((chip < last) & (chip > low)))
        def _():
            down(part, low).wait_send()
    for part in range(parts):
        for target in range(chips):
            to_core(part, target).wait_send()


def student_call(chips, vocabs, dense, peak_row, all_s, all_id, head):
    places, blocks, tokens, block = dense.shape
    count = places * vocabs
    depth, cols = head.shape
    rows = tokens // count
    span = 512
    tall = rows * depth // span
    halves = 2 if tall % 32 == 0 else 1
    tall = tall // halves
    parts = 4 if blocks % 32 == 0 else 1
    vmem = pl.BlockSpec(memory_space=pltpu.VMEM)
    dma = pltpu.SemaphoreType.DMA
    return pl.pallas_call(
        functools.partial(student_kernel, chips, vocabs),
        out_shape=jax.ShapeDtypeStruct((rows, depth), jnp.bfloat16),
        in_specs=[vmem, vmem, vmem, vmem, pl.BlockSpec(memory_space=pl.ANY)],
        out_specs=vmem,
        scratch_shapes=[
            pltpu.VMEM((depth, cols), head.dtype),
            pltpu.VMEM((chips, blocks, tokens, block), jnp.bfloat16),
            pltpu.VMEM((chips, blocks, tokens, block), jnp.bfloat16),
            pltpu.VMEM((chips, blocks, tokens, block), jnp.bfloat16),
            pltpu.VMEM((count, 8, tokens), jnp.float32),
            pltpu.VMEM((count, 8, tokens), jnp.float32),
            pltpu.VMEM((tokens, cols), jnp.float32),
            pltpu.VMEM((tokens, cols), jnp.bfloat16),
            pltpu.VMEM((tokens, depth), jnp.float32),
            pltpu.VMEM((halves, count, tall, span), jnp.float32),
            pltpu.VMEM((halves, count, tall, span), jnp.bfloat16),
            pltpu.VMEM((halves, chips, vocabs, tall, span), jnp.bfloat16),
            pltpu.VMEM((halves, chips * vocabs, tall, span), jnp.bfloat16),
            dma((cols // chunk_of(cols),)),
            dma((count,)), dma((count,)), dma((count,)), dma((count,)),
            dma((parts, chips)), dma((parts, chips)), dma((parts, chips)),
            dma((parts, chips)), dma((parts, chips)), dma((parts, chips)),
            dma((halves, chips)), dma((halves, chips)),
            dma((halves, chips * vocabs)), dma((halves, chips * vocabs)),
        ],
        compiler_params=pltpu.CompilerParams(
            collective_id=1, has_side_effects=True, vmem_limit_bytes=vmem_bytes
        ),
    )(dense, peak_row, all_s, all_id, head)


def on_device(
    teacher_hidden, teacher_head, map_dest, map_slot, map_weight,
    student_hidden, student_head, targets,
):
    places = lax.axis_size("dp")
    vocabs = lax.axis_size("vocab")
    chips = places // 2
    block = map_weight.shape[2]
    teacher_blocks, fan = map_dest.shape
    blocks = student_head.shape[1] // block
    logits, all_s, all_id, peak_row = teacher_call(
        chips, teacher_hidden, student_hidden, targets[None, :], teacher_head
    )
    tokens = logits.shape[0]
    weights = jnp.exp(logits - peak_row[0][:, None]).astype(jnp.bfloat16)
    terms = jnp.einsum(
        "gkc,krcd->krgd", weights.reshape(tokens, teacher_blocks, block), map_weight,
        preferred_element_type=jnp.float32,
    ).astype(jnp.bfloat16)
    items = teacher_blocks * fan
    goal = (map_dest * blocks + map_slot).reshape(items)
    marks = (jnp.arange(places * blocks, dtype=jnp.int32)[:, None] == goal[None, :]).astype(jnp.bfloat16)
    dense = jnp.dot(
        marks, terms.reshape(items, tokens * block), preferred_element_type=jnp.float32
    ).astype(jnp.bfloat16).reshape(places, blocks, tokens, block)
    return student_call(chips, vocabs, dense, peak_row, all_s, all_id, student_head)


def solution(mesh):
    placed = (
        P(("groups", "dp"), None),
        P(None, ("dp", "vocab")),
        P(("dp", "vocab"), None),
        P(("dp", "vocab"), None),
        P(("dp", "vocab"), None, None, None),
        P(("groups", "dp"), None),
        P(None, ("dp", "vocab")),
        P(("groups", "dp")),
    )
    return jax.shard_map(
        on_device,
        mesh=mesh,
        in_specs=placed,
        out_specs=P(("groups", "dp", "vocab"), None),
        check_vma=False,
    )
```

```python
import functools

import jax
import jax.numpy as jnp
from jax import lax
from jax.experimental import pallas as pl
from jax.experimental.pallas import tpu as pltpu
from jax.sharding import PartitionSpec as P

MESH = pl.DeviceIdType.MESH
hard_weight = 0.25
loss_scale = 64.0
vmem_bytes = 60 * 1024 * 1024


def chunk_of(cols):
    for size in (512, 256, 128):
        if cols % size == 0:
            return size
    return cols


def teacher_kernel(
    chips, own_t, own_s, own_id, head, logits, all_s, all_id, peak_row, peak_wide,
    held_t, held_s, held_id, tiles, tile_sem, send_sem, recv_sem, pass_sem, land_sem,
):
    place = lax.axis_index("dp")
    chip, core = place // 2, place % 2
    slots, width = tiles.shape[0], tiles.shape[2]
    steps = head.shape[1] // width

    def fetch(step, slot):
        return pltpu.make_async_copy(
            head.at[:, pl.ds(pl.multiple_of(step * width, width), width)],
            tiles.at[slot],
            tile_sem.at[slot],
        )

    for slot in range(min(slots, steps)):
        fetch(slot, slot).start()
    held_t[place] = own_t[...]
    held_s[place] = own_s[...]
    rows = own_t.shape[0]
    same = lax.broadcasted_iota(jnp.int32, (rows, rows), 0) == lax.broadcasted_iota(
        jnp.int32, (rows, rows), 1
    )
    held_id[place] = jnp.broadcast_to(
        jnp.sum(jnp.where(same, own_id[...], 0), axis=1, keepdims=True), held_id.shape[1:]
    )

    barrier = pltpu.get_barrier_semaphore()
    partner = chip * 2 + (1 - core)
    for hop in range(1, chips):
        other = (chip + hop) % chips * 2 + core
        pl.semaphore_signal(barrier, inc=1, device_id={"dp": other}, device_id_type=MESH)
    pl.semaphore_signal(barrier, inc=1, device_id={"dp": partner}, device_id_type=MESH)
    pl.semaphore_wait(barrier, chips)

    helds = (held_t, held_id, held_s)

    def across(kind, hop):
        return pltpu.make_async_remote_copy(
            src_ref=helds[kind].at[place],
            dst_ref=helds[kind].at[place],
            send_sem=send_sem.at[kind, hop],
            recv_sem=recv_sem.at[kind, hop],
            device_id={"dp": (chip + hop) % chips * 2 + core},
            device_id_type=MESH,
        )

    def between(kind, hop):
        block = (chip + chips - hop) % chips * 2 + core
        return pltpu.make_async_remote_copy(
            src_ref=helds[kind].at[block],
            dst_ref=helds[kind].at[block],
            send_sem=pass_sem.at[kind, hop],
            recv_sem=land_sem.at[kind, hop],
            device_id={"dp": partner},
            device_id_type=MESH,
        )

    for kind in range(2):
        for hop in range(1, chips):
            across(kind, hop).start()
        between(kind, 0).start()
    for hop in range(1, chips):
        across(0, hop).wait_recv()
        between(0, hop).start()
    for hop in range(1, chips):
        across(2, hop).start()
    between(2, 0).start()
    for hop in range(chips):
        between(0, hop).wait_recv()

    tokens = held_t.shape[0] * held_t.shape[1]

    def multiply(step, carry):
        slot = step % slots
        fetch(step, slot).wait()
        value = jnp.dot(
            held_t[...].reshape(tokens, held_t.shape[2]),
            tiles[slot],
            preferred_element_type=jnp.float32,
        )
        logits[:, pl.ds(pl.multiple_of(step * width, width), width)] = value
        for start in range(0, width, 128):
            carry = jnp.maximum(carry, value[:, start:start + 128])

        @pl.when(step + slots < steps)
        def _():
            fetch(step + slots, slot).start()

        return carry

    middle = steps // 2
    highest = jnp.full((tokens, 128), -jnp.inf, jnp.float32)
    highest = lax.fori_loop(0, middle, multiply, highest)
    for kind in (1, 2):
        for hop in range(1, chips):
            across(kind, hop).wait_recv()
            between(kind, hop).start()
    highest = lax.fori_loop(middle, steps, multiply, highest)
    for kind in (1, 2):
        for hop in range(chips):
            between(kind, hop).wait_recv()
    for kind in range(3):
        for hop in range(1, chips):
            across(kind, hop).wait_send()
        for hop in range(chips):
            between(kind, hop).wait_send()
    all_s[...] = held_s[...]
    all_id[...] = held_id[...]
    diagonal = lax.broadcasted_iota(jnp.int32, (tokens, tokens), 0) == lax.broadcasted_iota(
        jnp.int32, (tokens, tokens), 1
    )
    peak = jnp.max(highest, axis=1, keepdims=True)
    peak_wide[...] = jnp.broadcast_to(peak, peak_wide.shape)
    peak_row[...] = jnp.broadcast_to(
        jnp.sum(jnp.where(diagonal, peak, 0.0), axis=0, keepdims=True), peak_row.shape
    )


def teacher_call(chips, own_t, own_s, own_id, head):
    depth, cols = head.shape
    width = chunk_of(cols)
    slots = min(8, cols // width)
    places = chips * 2
    rows = own_t.shape[0]
    vmem = pl.BlockSpec(memory_space=pltpu.VMEM)
    return pl.pallas_call(
        functools.partial(teacher_kernel, chips),
        out_shape=(
            jax.ShapeDtypeStruct((places * rows, cols), jnp.float32),
            jax.ShapeDtypeStruct((places,) + own_s.shape, own_s.dtype),
            jax.ShapeDtypeStruct((places, rows, 128), own_id.dtype),
            jax.ShapeDtypeStruct((8, places * rows), jnp.float32),
            jax.ShapeDtypeStruct((places * rows, 128), jnp.float32),
        ),
        in_specs=[vmem, vmem, vmem, pl.BlockSpec(memory_space=pl.ANY)],
        out_specs=(vmem,) * 5,
        scratch_shapes=[
            pltpu.VMEM((places,) + own_t.shape, own_t.dtype),
            pltpu.VMEM((places,) + own_s.shape, own_s.dtype),
            pltpu.VMEM((places, rows, 128), own_id.dtype),
            pltpu.VMEM((slots, depth, width), head.dtype),
            pltpu.SemaphoreType.DMA((slots,)),
            pltpu.SemaphoreType.DMA((3, chips)),
            pltpu.SemaphoreType.DMA((3, chips)),
            pltpu.SemaphoreType.DMA((3, chips)),
            pltpu.SemaphoreType.DMA((3, chips)),
        ],
        compiler_params=pltpu.CompilerParams(
            collective_id=0, has_side_effects=True, vmem_limit_bytes=vmem_bytes
        ),
    )(own_t, own_s, own_id, head)


def map_kernel(goal, logits, peak, weight, dense, total):
    step = pl.program_id(0)
    group, fan, block = weight.shape[0], weight.shape[1], weight.shape[2]

    @pl.when(step == 0)
    def _():
        def clear(index, carry):
            total[index] = jnp.zeros(total.shape[1:], total.dtype)
            return carry

        lax.fori_loop(0, total.shape[0], clear, 0, unroll=4)

    for inner in range(group):
        part = jnp.exp(logits[:, inner * block:(inner + 1) * block] - peak[...]).astype(jnp.bfloat16)
        terms = [
            jnp.dot(part, weight[inner, entry], preferred_element_type=jnp.float32).astype(jnp.bfloat16)
            for entry in range(fan)
        ]
        for entry in range(fan):
            spot = goal[(step * group + inner) * fan + entry]
            total[spot] += terms[entry].astype(jnp.float32)

    @pl.when(step == pl.num_programs(0) - 1)
    def _():
        def narrow(index, carry):
            dense[index] = total[index].astype(dense.dtype)
            return carry

        lax.fori_loop(0, total.shape[0], narrow, 0, unroll=4)


def map_call(goal, logits, peak, weight, spots):
    teacher_blocks, fan, block, wide = weight.shape
    tokens = logits.shape[0]
    group = 8 if teacher_blocks % 8 == 0 else teacher_blocks
    return pl.pallas_call(
        map_kernel,
        grid=(teacher_blocks // group,),
        out_shape=jax.ShapeDtypeStruct((spots, tokens, wide), jnp.bfloat16),
        in_specs=[
            pl.BlockSpec(memory_space=pltpu.SMEM),
            pl.BlockSpec((tokens, group * block), lambda step: (0, step)),
            pl.BlockSpec((tokens, block), lambda step: (0, 0)),
            pl.BlockSpec((group, fan, block, wide), lambda step: (step, 0, 0, 0)),
        ],
        out_specs=pl.BlockSpec((spots, tokens, wide), lambda step: (0, 0, 0)),
        scratch_shapes=[pltpu.VMEM((spots, tokens, wide), jnp.float32)],
        compiler_params=pltpu.CompilerParams(vmem_limit_bytes=vmem_bytes),
    )(goal, logits, peak, weight)


def student_kernel(
    chips, vocabs, dense, peak_row, all_s, all_id, head, out,
    whole, summed, up_in, down_in, peaks, stats, logits, grad, product, partial, sent, given, landed,
    tile_sem, peak_send, peak_recv, stat_send, stat_recv, core_send, core_recv,
    up_send, up_recv, down_send, down_recv, give_send, give_recv, grad_send, grad_recv,
):
    place, vocab = lax.axis_index("dp"), lax.axis_index("vocab")
    chip, core = place // 2, place % 2
    partner = chip * 2 + (1 - core)
    count = chips * 2 * vocabs
    me = place * vocabs + vocab
    blocks, tokens, block = summed.shape[1:]
    depth, cols = head.shape
    width = chunk_of(cols)
    steps = cols // width
    last = chips - 1
    parts = core_send.shape[0]
    share_of = blocks // parts

    def fetch(step):
        at = pl.ds(pl.multiple_of(step * width, width), width)
        return pltpu.make_async_copy(head.at[:, at], whole.at[:, at], tile_sem.at[step])

    for step in range(steps):
        fetch(step).start()
    peaks[me] = peak_row[...]

    def every(body):
        lax.fori_loop(1, count, lambda hop, carry: (body(hop), carry)[1], 0)

    def peer(hop):
        other = (me + hop) % count
        return {"dp": other // vocabs, "vocab": other % vocabs}

    barrier = pltpu.get_barrier_semaphore()
    every(lambda hop: pl.semaphore_signal(barrier, inc=1, device_id=peer(hop), device_id_type=MESH))
    pl.semaphore_wait(barrier, count - 1)

    def share(ref, send_sem, recv_sem):
        def one(hop):
            return pltpu.make_async_remote_copy(
                src_ref=ref.at[me], dst_ref=ref.at[me],
                send_sem=send_sem.at[hop], recv_sem=recv_sem.at[hop],
                device_id=peer(hop), device_id_type=MESH,
            )
        return one

    share_peak = share(peaks, peak_send, peak_recv)
    share_stat = share(stats, stat_send, stat_recv)
    every(lambda hop: share_peak(hop).start())

    order = []
    for near in range((chips + 1) // 2):
        order += [last - near] + ([near] if near != last - near else [])

    def to_core(part, target):
        return pltpu.make_async_remote_copy(
            src_ref=dense.at[target * 2 + 1 - core, pl.ds(part * share_of, share_of)],
            dst_ref=summed.at[target, pl.ds(part * share_of, share_of)],
            send_sem=core_send.at[part, target], recv_sem=core_recv.at[part, target],
            device_id={"dp": partner}, device_id_type=MESH,
        )

    def up(part, target):
        return pltpu.make_async_remote_copy(
            src_ref=summed.at[target, pl.ds(part * share_of, share_of)],
            dst_ref=up_in.at[target, pl.ds(part * share_of, share_of)],
            send_sem=up_send.at[part, target], recv_sem=up_recv.at[part, target],
            device_id={"dp": (chip + 1) % chips * 2 + core}, device_id_type=MESH,
        )

    def down(part, target):
        return pltpu.make_async_remote_copy(
            src_ref=summed.at[target, pl.ds(part * share_of, share_of)],
            dst_ref=down_in.at[target, pl.ds(part * share_of, share_of)],
            send_sem=down_send.at[part, target], recv_sem=down_recv.at[part, target],
            device_id={"dp": (chip + last) % chips * 2 + core}, device_id_type=MESH,
        )

    for target in order:
        to_core(0, target).start()

    eye = lax.broadcasted_iota(jnp.int32, (tokens, tokens), 0) == lax.broadcasted_iota(
        jnp.int32, (tokens, tokens), 1
    )

    def column(row):
        return jnp.sum(jnp.where(eye, row, 0.0), axis=1, keepdims=True)

    def row_of(col):
        return jnp.sum(jnp.where(eye, col, 0.0), axis=0, keepdims=True)

    def add_rows(index, total):
        tile = dense[index // blocks, index % blocks]
        return total + tile.astype(jnp.float32)

    row_total = lax.fori_loop(
        0, 2 * chips * blocks, add_rows, jnp.zeros((tokens, block), jnp.float32)
    )
    every(lambda hop: share_peak(hop).wait())
    peak = column(jnp.max(peaks[:, 0:1, :], axis=0))
    own_scale = jnp.exp(column(peaks[me, 0:1, :]) - peak)
    partner_scale = jnp.exp(column(peaks[partner * vocabs + vocab, 0:1, :]) - peak)
    term_total = own_scale * jnp.sum(row_total, axis=1, keepdims=True)
    own_wide = jnp.broadcast_to(own_scale, (tokens, block))
    partner_wide = jnp.broadcast_to(partner_scale, (tokens, block))

    def combine(part):
        for target in order:
            to_core(part, target).wait_recv()

            def one(index, carry):
                summed[target, index] = (
                    dense[target * 2 + core, index].astype(jnp.float32) * own_wide
                    + summed[target, index].astype(jnp.float32) * partner_wide
                ).astype(summed.dtype)
                return carry

            lax.fori_loop(part * share_of, (part + 1) * share_of, one, 0)

    def multiply(step, carry):
        fetch(step).wait()
        at = pl.ds(pl.multiple_of(step * width, width), width)
        logits[:, at] = jnp.dot(
            all_s[...].reshape(tokens, depth), whole[:, at], preferred_element_type=jnp.float32
        )
        return carry

    def add_in(part, target, ref):
        def one(index, carry):
            summed[target, index] = (
                summed[target, index].astype(jnp.float32) + ref[target, index].astype(jnp.float32)
            ).astype(summed.dtype)
            return carry

        lax.fori_loop(part * share_of, (part + 1) * share_of, one, 0)

    turns = [(part, turn) for part in range(parts) for turn in range(last)]

    def hop_up(at):
        part, high = turns[at][0], last - turns[at][1]

        @pl.when(chip == 0)
        def _():
            if at >= 2:
                up(turns[at - 2][0], last - turns[at - 2][1]).wait_send()
            up(part, high).start()

        if high > 1:
            @pl.when((chip > 0) & (chip < high))
            def _():
                up(part, high).wait_recv()
                add_in(part, high, up_in)
                up(part, high).start()

    def hop_down(at):
        part, low = turns[at]

        @pl.when(chip == last)
        def _():
            if at >= 2:
                down(*turns[at - 2]).wait_send()
            down(part, low).start()

        if low < last - 1:
            @pl.when((chip < last) & (chip > low))
            def _():
                down(part, low).wait_recv()
                add_in(part, low, down_in)
                down(part, low).start()

    def hop(at):
        pl.when(chip * 2 < chips)(lambda: hop_up(at))
        hop_down(at)
        pl.when(chip * 2 >= chips)(lambda: hop_up(at))

    ids = all_id[...].reshape(tokens, block)
    lanes = lax.broadcasted_iota(jnp.int32, (tokens, block), 1) + me * cols

    def totals():
        target_total = column(jnp.sum(stats[:, 0:1, :], axis=0))
        peak_all = jnp.max(stats[:, 1:2, :], axis=0)
        student_total = column(
            jnp.sum(stats[:, 2:3, :] * jnp.exp(stats[:, 1:2, :] - peak_all), axis=0)
        )
        return tuple(
            jnp.broadcast_to(value, (tokens, block))
            for value in (
                column(peak_all),
                loss_scale / student_total,
                loss_scale * (1.0 - hard_weight) / target_total,
            )
        )

    halves = partial.shape[0]
    rows, span = out.shape[0], partial.shape[3]
    pieces = depth // span
    per_half = pieces // halves

    def finish(part, wide):
        peak_wide, student_gain, target_gain = wide
        for target in range(chips):
            if target > 0:
                @pl.when(chip == target)
                def _():
                    up(part, target).wait_recv()
            if target < last:
                @pl.when(chip == target)
                def _():
                    down(part, target).wait_recv()

        def one(index, carry):
            mapped = summed[chip, index].astype(jnp.float32)
            mapped = mapped + jnp.where(chip > 0, up_in[chip, index].astype(jnp.float32), 0.0)
            mapped = mapped + jnp.where(chip < last, down_in[chip, index].astype(jnp.float32), 0.0)
            at = pl.ds(pl.multiple_of(index * block, block), block)
            student = jnp.exp(logits[:, at] - peak_wide) * student_gain
            hits = jnp.where(ids == lanes + index * block, loss_scale * hard_weight, 0.0)
            grad[:, at] = (student - mapped * target_gain - hits).astype(grad.dtype)
            return carry

        lax.fori_loop(part * share_of, (part + 1) * share_of, one, 0)

    def piece_of(part, piece):
        across = slice(part * share_of * block, (part + 1) * share_of * block)
        return lax.dot_general(
            grad[:, across], whole[piece * span:(piece + 1) * span, across],
            (((1,), (1,)), ((), ())), preferred_element_type=jnp.float32,
        )

    def accumulate(part):
        for piece in range(pieces):
            at = slice(piece * span, (piece + 1) * span)
            value = piece_of(part, piece)
            product[:, at] = value if part == 0 else product[:, at] + value

    def give(half, target):
        return pltpu.make_async_remote_copy(
            src_ref=sent.at[half, pl.ds((target * 2 + 1 - core) * vocabs, vocabs)],
            dst_ref=given.at[half, target],
            send_sem=give_send.at[half, target], recv_sem=give_recv.at[half, target],
            device_id={"dp": partner}, device_id_type=MESH,
        )

    column_me = chip * vocabs + vocab
    column_count = chips * vocabs

    def owner_of(step):
        other = (column_me + step) % column_count
        return other // vocabs, other % vocabs

    def share_grad(half, step):
        target, side = owner_of(step)
        return pltpu.make_async_remote_copy(
            src_ref=sent.at[half, (target * 2 + core) * vocabs + side], dst_ref=landed.at[half, step],
            send_sem=grad_send.at[half, step], recv_sem=grad_recv.at[half, step],
            device_id={"dp": target * 2 + core, "vocab": side}, device_id_type=MESH,
        )

    combine(0)
    for part in range(1, parts):
        for target in order:
            to_core(part, target).start()
    busy = max(1, (len(turns) + 1) // 2)
    done = 0
    wide = None
    accumulated = 0
    for at, (part, turn) in enumerate(turns):
        hop(at)
        if at < busy:
            until = steps * (at + 1) // busy
            lax.fori_loop(done, until, multiply, 0)
            done = until
        if at == busy - 1:
            own_peak = jnp.max(logits[...], axis=1, keepdims=True)
            own_sum = jnp.sum(jnp.exp(logits[...] - own_peak), axis=1, keepdims=True)
            stats[me, 0:1, :] = row_of(term_total)
            stats[me, 1:2, :] = row_of(own_peak)
            stats[me, 2:3, :] = row_of(own_sum)
            stats[me, 3:8, :] = jnp.zeros((5, tokens), jnp.float32)
            every(lambda step: share_stat(step).start())
        if turn == last - 1 and part + 1 < parts:
            combine(part + 1)
        if at >= busy + last - 1 and at < len(turns) - 1 and accumulated < part:
            if wide is None:
                every(lambda step: share_stat(step).wait())
                wide = totals()
            finish(accumulated, wide)
            accumulate(accumulated)
            accumulated += 1
    if wide is None:
        every(lambda step: share_stat(step).wait())
        wide = totals()
    for part in range(accumulated, parts - 1):
        finish(part, wide)
        accumulate(part)
    finish(parts - 1, wide)

    for half in range(halves):
        for inner in range(per_half):
            piece = half * per_half + inner
            value = piece_of(parts - 1, piece)
            if parts > 1:
                value = value + product[:, piece * span:(piece + 1) * span]
            for owner in range(count):
                partial[half, owner, inner * rows:(inner + 1) * rows, :] = value[owner * rows:(owner + 1) * rows, :]
        for target in range(chips):
            first = (target * 2 + 1 - core) * vocabs
            for side in range(vocabs):
                sent[half, first + side] = partial[half, first + side].astype(sent.dtype)
            give(half, target).start()

    for half in range(halves):
        for target in range(chips):
            give(half, target).wait_recv()

        def pass_on(step, carry):
            target, side = owner_of(step)
            owner = (target * 2 + core) * vocabs + side
            sent[half, owner] = (
                partial[half, owner] + given[half, target, side].astype(jnp.float32)
            ).astype(sent.dtype)
            share_grad(half, step).start()
            return carry

        lax.fori_loop(1, column_count, pass_on, 0)

    for half in range(halves):
        def arrive(step, total):
            share_grad(half, step).wait_recv()
            return total + landed[half, step].astype(jnp.float32)

        total = lax.fori_loop(
            1, column_count, arrive, partial[half, me] + given[half, chip, vocab].astype(jnp.float32)
        )
        for inner in range(per_half):
            piece = half * per_half + inner
            out[:, piece * span:(piece + 1) * span] = total[
                inner * rows:(inner + 1) * rows, :
            ].astype(out.dtype)

    for half in range(halves):
        for target in range(chips):
            give(half, target).wait_send()
        lax.fori_loop(1, column_count, lambda step, carry: (share_grad(half, step).wait_send(), carry)[1], 0)
    for at, (part, turn) in enumerate(turns):
        high, low = last - turn, turn
        late = at >= len(turns) - 2

        @pl.when((chip < high) if late else ((chip > 0) & (chip < high)))
        def _():
            up(part, high).wait_send()

        @pl.when((chip > low) if late else ((chip < last) & (chip > low)))
        def _():
            down(part, low).wait_send()
    for part in range(parts):
        for target in range(chips):
            to_core(part, target).wait_send()


def student_call(chips, vocabs, dense, peak_row, all_s, all_id, head):
    places, blocks, tokens, block = dense.shape
    count = places * vocabs
    depth, cols = head.shape
    rows = tokens // count
    span = 512
    tall = rows * depth // span
    halves = 2 if tall % 32 == 0 else 1
    tall = tall // halves
    parts = 4 if blocks % 32 == 0 else 1
    vmem = pl.BlockSpec(memory_space=pltpu.VMEM)
    dma = pltpu.SemaphoreType.DMA
    return pl.pallas_call(
        functools.partial(student_kernel, chips, vocabs),
        out_shape=jax.ShapeDtypeStruct((rows, depth), jnp.bfloat16),
        in_specs=[vmem, vmem, vmem, vmem, pl.BlockSpec(memory_space=pl.ANY)],
        out_specs=vmem,
        scratch_shapes=[
            pltpu.VMEM((depth, cols), head.dtype),
            pltpu.VMEM((chips, blocks, tokens, block), jnp.bfloat16),
            pltpu.VMEM((chips, blocks, tokens, block), jnp.bfloat16),
            pltpu.VMEM((chips, blocks, tokens, block), jnp.bfloat16),
            pltpu.VMEM((count, 8, tokens), jnp.float32),
            pltpu.VMEM((count, 8, tokens), jnp.float32),
            pltpu.VMEM((tokens, cols), jnp.float32),
            pltpu.VMEM((tokens, cols), jnp.bfloat16),
            pltpu.VMEM((tokens, depth), jnp.float32),
            pltpu.VMEM((halves, count, tall, span), jnp.float32),
            pltpu.VMEM((halves, count, tall, span), jnp.bfloat16),
            pltpu.VMEM((halves, chips, vocabs, tall, span), jnp.bfloat16),
            pltpu.VMEM((halves, chips * vocabs, tall, span), jnp.bfloat16),
            dma((cols // chunk_of(cols),)),
            dma((count,)), dma((count,)), dma((count,)), dma((count,)),
            dma((parts, chips)), dma((parts, chips)), dma((parts, chips)),
            dma((parts, chips)), dma((parts, chips)), dma((parts, chips)),
            dma((halves, chips)), dma((halves, chips)),
            dma((halves, chips * vocabs)), dma((halves, chips * vocabs)),
        ],
        compiler_params=pltpu.CompilerParams(
            collective_id=1, has_side_effects=True, vmem_limit_bytes=vmem_bytes
        ),
    )(dense, peak_row, all_s, all_id, head)


def on_device(
    teacher_hidden, teacher_head, map_dest, map_slot, map_weight,
    student_hidden, student_head, targets,
):
    places = lax.axis_size("dp")
    vocabs = lax.axis_size("vocab")
    chips = places // 2
    block = map_weight.shape[2]
    teacher_blocks, fan = map_dest.shape
    blocks = student_head.shape[1] // block
    logits, all_s, all_id, peak_row, peak_wide = teacher_call(
        chips, teacher_hidden, student_hidden, targets[None, :], teacher_head
    )
    goal = (map_dest * blocks + map_slot).reshape(teacher_blocks * fan)
    dense = map_call(goal, logits, peak_wide, map_weight, places * blocks)
    dense = dense.reshape((places, blocks) + dense.shape[1:])
    return student_call(chips, vocabs, dense, peak_row, all_s, all_id, student_head)


def solution(mesh):
    placed = (
        P(("groups", "dp"), None),
        P(None, ("dp", "vocab")),
        P(("dp", "vocab"), None),
        P(("dp", "vocab"), None),
        P(("dp", "vocab"), None, None, None),
        P(("groups", "dp"), None),
        P(None, ("dp", "vocab")),
        P(("groups", "dp")),
    )
    return jax.shard_map(
        on_device,
        mesh=mesh,
        in_specs=placed,
        out_specs=P(("groups", "dp", "vocab"), None),
        check_vma=False,
    )
```
